512 devices in a mesh: chan: 128 (over z, x, core), blk: 4 (over y).
Axes of the slice: x: 4, y: 4, z: 16, core: 2. Of those that a mesh axis runs over, the one named last changes fastest.
Arguments:
- omega: float32 [128, 576, 576], P('chan', 'blk'), may hold values from -0.25 to 0.25
- hamiltonian: float32 [128, 576, 576], P('chan', 'blk'), may hold values from -6 to 6
- pair_occ: float32 [128, 576], P('chan'), may hold values from -1 to 1
- cross_occ: float32 [128, 576], P('chan'), may hold values from -1 to 1
- block_size: int32 [128], P('chan'), may hold values from 288 to 576
- jlabel: int32 [128], replicated, may hold values from 0 to 127
- family: int32 [128], replicated, may hold values from 0 to 3
- sixj: float32 [128, 128], replicated, may hold values from -1 to 1
- column_map: int32 [576], replicated, may hold values from 0 to 575, each once
Outputs:
- evolved: float32 [128, 576, 576], P('chan', 'blk')
The draws below stay inside these ranges and needn't reach their ends.
Inputs may be any that keep to these rules, and one draw needn't show every extreme that they name: `column_map`: a permutation of 0 to 575.
All inputs are finite; a program needn't handle non-finite values.
Results may differ from the reference program's by a relative error of at most 0.0032.
Values may be sent and summed in bfloat16 or wider, within the bound.
A program may use at most 64 MiB of HBM per device.

```python
import jax
import jax.numpy as jnp
from jax import lax

P_SIZE = 576
FAMILIES = 4
NCHAN = 128
JMAX = 128


def set_ends(result, stream_key, least, top_value):
    longest = result.shape.index(max(result.shape))
    spots = []
    for shift in (0, 1):
        where = [jax.random.randint(jax.random.fold_in(stream_key, axis), (), 0, length) for axis, length in enumerate(result.shape)]
        where[longest] = (where[longest] + shift) % result.shape[longest]
        spots.append(tuple(where))
    return result.at[spots[0]].set(least).at[spots[1]].set(top_value)


def block_scale(rng, shape, split, low, top_value):
    def one(axis_at, blocks):
        draws = jax.random.uniform(jax.random.fold_in(jax.random.fold_in(rng, 6), axis_at), (blocks,), jnp.float32, low / len(split), top_value / len(split))
        return jnp.repeat(jnp.exp(draws), shape[axis_at] // blocks).reshape((-1,) + (1,) * (len(shape) - axis_at - 1))

    loudness = one(*split[0])
    for cut in split[1:]:
        loudness = loudness * one(*cut)
    return loudness


def bell_draw(key, dims, spread, limit, split=(), kind=jnp.bfloat16):
    drawn = spread * jax.random.normal(key, dims, jnp.float32)
    if split:
        drawn = drawn * block_scale(key, dims, split, -0.22, 0.18)
    return jnp.clip(drawn, -limit, limit).astype(kind)


def setup_inputs(seed: int = 0) -> dict:
    splits = jax.random.split(jax.random.key(seed), 10)
    omega = bell_draw(splits[0], (NCHAN, P_SIZE, P_SIZE), P_SIZE ** -0.5, 0.25, ((0, 128), (1, 4)), jnp.float32)
    hamiltonian = bell_draw(splits[1], (NCHAN, P_SIZE, P_SIZE), 1.0, 6.0, ((0, 128), (1, 4)), jnp.float32)
    pair_occ = jnp.clip(jax.random.uniform(splits[2], (NCHAN, P_SIZE), jnp.float32, -1.0, 1.0) * block_scale(splits[2], (NCHAN, P_SIZE), ((0, 128),), -0.4, 0.0), -1.0, 1.0)
    cross_occ = jnp.clip(jax.random.uniform(splits[3], (NCHAN, P_SIZE), jnp.float32, -1.0, 1.0) * block_scale(splits[3], (NCHAN, P_SIZE), ((0, 128),), -0.4, 0.0), -1.0, 1.0)
    block_size = set_ends(jax.random.randint(splits[4], (NCHAN,), P_SIZE // 2, P_SIZE + 1), jax.random.fold_in(splits[4], 1), P_SIZE // 2, P_SIZE).astype(jnp.int32)
    jlabel = set_ends(jax.random.randint(splits[5], (NCHAN,), 0, JMAX), jax.random.fold_in(splits[5], 1), 0, JMAX - 1).astype(jnp.int32)
    family = set_ends(jax.random.randint(splits[6], (NCHAN,), 0, FAMILIES), jax.random.fold_in(splits[6], 1), 0, FAMILIES - 1).astype(jnp.int32)
    sixj = bell_draw(splits[7], (JMAX, JMAX), (NCHAN // FAMILIES) ** -0.5, 1.0, (), jnp.float32)
    column_map = jax.random.permutation(splits[8], P_SIZE).astype(jnp.int32)
    return dict(omega=omega, hamiltonian=hamiltonian, pair_occ=pair_occ, cross_occ=cross_occ, block_size=block_size, jlabel=jlabel, family=family, sixj=sixj, column_map=column_map)


exact_mode = lax.Precision.HIGHEST


def rounded(value):
    return lax.optimization_barrier(value.astype(jnp.bfloat16)).astype(jnp.float32)


def commute(operand_left, operand_right, weights):
    scaled_left = rounded(operand_left * weights[:, None, :])
    scaled_right = rounded(operand_right * weights[:, None, :])
    plain_left = rounded(operand_left)
    plain_right = rounded(operand_right)
    forward_term = jnp.einsum('cik,ckj->cij', scaled_left, plain_right, precision=exact_mode)
    reverse_term = jnp.einsum('cik,ckj->cij', scaled_right, plain_left, precision=exact_mode)
    return forward_term - reverse_term


def reference(omega, hamiltonian, pair_occ, cross_occ, block_size, jlabel, family, sixj, column_map):
    positions = jnp.arange(P_SIZE, dtype=jnp.int32)
    inside_block = (positions[None, :, None] < block_size[:, None, None]) & (positions[None, None, :] < block_size[:, None, None])
    window_mask = inside_block.astype(jnp.float32)
    generator = omega * window_mask
    start_ham = hamiltonian * window_mask
    kindred = (family[:, None] == family[None, :]).astype(jnp.float32)
    mixing = sixj[jlabel[:, None], jlabel[None, :]] * kindred
    inverse_map = jnp.argsort(column_map).astype(jnp.int32)

    def recouple(operand):
        return jnp.einsum('kc,cij->kij', mixing, operand[:, :, column_map], precision=exact_mode)

    def restore(operand):
        return jnp.einsum('ck,cij->kij', mixing, operand, precision=exact_mode)[:, :, inverse_map]

    gen_cross = recouple(generator)
    ham_cross = recouple(start_ham)
    first_pp = commute(generator, start_ham, pair_occ)
    first_cc = commute(gen_cross, ham_cross, cross_occ)
    eta = first_pp + restore(first_cc)
    eta_cross = recouple(eta)
    second = commute(generator, eta, pair_occ) + restore(commute(gen_cross, eta_cross, cross_occ))
    return (start_ham + eta + 0.5 * second) * window_mask
```

```python
import math

import jax
import jax.numpy as jnp
from jax import lax
from jax.experimental import pallas as pl
from jax.experimental.pallas import tpu as pltpu
from jax.sharding import PartitionSpec as P

F32 = jnp.float32
BF16 = jnp.bfloat16
I32 = jnp.int32
MESH = pl.DeviceIdType.MESH

C = 128
L = 8
Y = 4
ROWS = 144
WIDTH = 576
WIDE = 640
PER = 3
OWNERS = 112
WORDS = OWNERS * PER
TAIL = 288
LAST = 328

G, H, PP, CC, SO = range(5)
GB, HB, EB, RB, SB = range(5)
YG, YH, YGC, YHC, YE, YEC = range(6)

FLOOR = -126.0
OUT_TOP = (0.25, 6.0, 2.0**11, 2.0**26, 2.0**55)
BACK_TOP = (2.0**6, 2.0**11, 2.0**40, 2.0**34, 2.0**63)


def per_octave(top):
    return 32766.0 / (math.log2(top) - FLOOR)


def dot(a, b):
    return jnp.dot(a, b, preferred_element_type=F32)


def halves(value):
    high = value.astype(BF16)
    return high, (value - high.astype(F32)).astype(BF16)


def encode(value, top):
    scale = per_octave(top)
    size = jnp.maximum(jnp.abs(value), 2.0**FLOOR)
    code = jnp.minimum(jnp.round((jnp.log2(size) - FLOOR) * scale), 32767.0)
    return jnp.where(value < 0, -code, code).astype(I32)


def decode(code, top):
    value = code.astype(F32)
    size = jnp.exp2(jnp.abs(value) * (1.0 / per_octave(top)) + FLOOR)
    size = jnp.where(value < 0, -size, size)
    return jnp.where(value == 0, 0.0, size)


def pack(first, second):
    return lax.shift_left(first, 16) | (second & 0xFFFF)


def unpack(word):
    first = lax.shift_right_arithmetic(word, 16)
    return first, lax.shift_right_arithmetic(lax.shift_left(word, 16), 16)


def kernel(
    omega_hbm, ham_hbm, pair_w, cross_w, block, jrow, frow, sixj, cmap,
    out,
    os_ref, or_ref, bs_ref, br_ref,
    full, perm, unperm, mix_hi, mix_lo, rev_hi, rev_lo, sq_hi, sq_lo,
    wide_ref, block_ref, tail_ref, x_hi, x_lo,
    gen_ref, ham_ref, pp_ref, comb_ref, gen_s, ham_s, gc_s, hc_s, eta_ref,
    in_sem, os_sem, or_sem, bs_sem, br_sem, ys_sem, yr_sem,
):
    me = lax.axis_index("chan")
    y = lax.axis_index("blk")
    z = me // L
    lane = lax.rem(me, L)
    place = lax.rem(lane - z - 1 + 3 * L, L)
    owns = place < L - 1
    idle = place == L - 1
    mine = z * (L - 1) + jnp.minimum(place, L - 2)
    idle_n = place // (L - 1)
    y_next = lax.rem(y + 1, Y)
    y_last = lax.rem(y + Y - 1, Y)

    barrier = pltpu.get_barrier_semaphore()

    def greet(step, _):
        to = lax.rem(me + step, C)
        pl.semaphore_signal(barrier, inc=1, device_id={"chan": to}, device_id_type=MESH)
        return 0

    lax.fori_loop(1, C, greet, 0)
    for other in (y_next, y_last):
        pl.semaphore_signal(barrier, inc=1, device_id={"blk": other}, device_id_type=MESH)

    omega_copy = pltpu.make_async_copy(omega_hbm, gen_ref, in_sem.at[0])
    ham_copy = pltpu.make_async_copy(ham_hbm, ham_ref, in_sem.at[1])
    omega_copy.start()
    ham_copy.start()

    def rows(index):
        return pl.ds(index * PER, PER)

    def start_out(t):
        first = z * (L - 1) + place + 1 - idle_n

        def one(step, _):
            owner = lax.rem(first + step, OWNERS)
            plane = owner // (L - 1)
            to = plane * L + lax.rem(plane + 1 + lax.rem(owner, L - 1), L)
            pltpu.make_async_remote_copy(
                src_ref=os_ref.at[t, rows(owner)], dst_ref=or_ref.at[t, rows(me)],
                send_sem=os_sem.at[t], recv_sem=or_sem.at[t],
                device_id={"chan": to}, device_id_type=MESH,
            ).start()
            return 0

        lax.fori_loop(0, OWNERS - 1 + idle_n, one, 0)

        @pl.when(owns)
        def _():
            pltpu.make_async_copy(
                os_ref.at[t, rows(mine)], or_ref.at[t, rows(me)], or_sem.at[t]
            ).start()

    def start_back(t):
        def one(step, _):
            to = lax.rem(me + step, C)
            pltpu.make_async_remote_copy(
                src_ref=bs_ref.at[t, rows(to)], dst_ref=br_ref.at[t, rows(mine)],
                send_sem=bs_sem.at[t], recv_sem=br_sem.at[t],
                device_id={"chan": to}, device_id_type=MESH,
            ).start()
            return 0

        lax.fori_loop(1, C, one, 0)
        pltpu.make_async_copy(
            bs_ref.at[t, rows(me)], br_ref.at[t, rows(mine)], br_sem.at[t]
        ).start()

    def wait_rows(ref, count, sem):
        part = ref.at[pl.ds(0, count)]
        pltpu.make_async_copy(part, part, sem).wait()

    def send(t, value):
        code = encode(value, OUT_TOP[t])
        for b in range(2):
            os_ref[t, ROWS * b : ROWS * (b + 1), :] = pack(
                code[:, 256 * b : 256 * b + 128], code[:, 256 * b + 128 : 256 * b + 256]
            )
        tail_ref[...] = code[0:72, 512:WIDE] + pltpu.roll(code[72:144, 512:WIDE], 64, 1)
        os_ref[t, TAIL:LAST, :] = pack(tail_ref[0:40, :], tail_ref[32:72, :])
        os_ref[t, LAST:WORDS, :] = jnp.zeros((WORDS - LAST, 128), I32)

    def arrived(t):
        wait_rows(or_ref.at[t], C * PER, or_sem.at[t])
        for j in range(PER):
            for k, code in enumerate(unpack(or_ref[t, pl.ds(j, C, stride=PER), :])):
                at = slice(256 * j + 128 * k, 256 * j + 128 * (k + 1))
                x_hi[:, at], x_lo[:, at] = halves(decode(code, OUT_TOP[t]))

    def times(high, low):
        return dot(high[...], x_hi[...]) + (dot(high[...], x_lo[...]) + dot(low[...], x_hi[...]))

    def send_mixed(t, value):
        code = encode(value, BACK_TOP[t])
        for j in range(PER):
            bs_ref[t, pl.ds(j, C, stride=PER), :] = pack(
                code[:, 256 * j : 256 * j + 128], code[:, 256 * j + 128 : 256 * j + 256]
            )
        start_back(t)

    def take_block(t):
        wait_rows(br_ref.at[t], WORDS, br_sem.at[t])
        top = BACK_TOP[t]
        for b in range(2):
            for k, code in enumerate(unpack(br_ref[t, ROWS * b : ROWS * (b + 1), :])):
                block_ref[:, 256 * b + 128 * k : 256 * b + 128 * (k + 1)] = decode(code, top)
        first, second = unpack(br_ref[t, TAIL:LAST, :])
        tail_ref[0:40, :] = first
        tail_ref[32:72, :] = second
        tail = decode(tail_ref[...], top)
        block_ref[0:72, 512:576] = tail[:, 0:64]
        block_ref[72:144, 512:576] = pltpu.roll(tail, 64, 1)[:, 0:64]
        return block_ref[...]

    def permuted(value, matrix):
        high, low = halves(value)
        return dot(high, matrix[...]) + dot(low, matrix[...])

    CUT = 80

    def y_copy(g, k, rows, to):
        return pltpu.make_async_remote_copy(
            src_ref=rows, dst_ref=rows,
            send_sem=ys_sem.at[g, k], recv_sem=yr_sem.at[g, k],
            device_id={"blk": to}, device_id_type=MESH,
        )

    def own_rows(g, who):
        return full.at[g, who]

    def upper(g, who):
        return full.at[g, who, pl.ds(0, CUT)]

    def lower(g, who):
        return full.at[g, who, pl.ds(CUT, ROWS - CUT)]

    def y_send(g):
        y_copy(g, 0, own_rows(g, y), y_next).start()
        y_copy(g, 1, own_rows(g, y), y_last).start()

    def y_start(g, value):
        full[g, y] = value
        y_send(g)

    def y_relay(g):
        y_copy(g, 0, own_rows(g, y_last), y_next).wait_recv()
        y_copy(g, 2, upper(g, y_last), y_next).start()
        y_copy(g, 1, own_rows(g, y_next), y_last).wait_recv()
        y_copy(g, 3, lower(g, y_next), y_last).start()

    def y_finish(g):
        far = lax.rem(y + 2, Y)
        y_copy(g, 2, upper(g, far), y_next).wait_recv()
        y_copy(g, 3, lower(g, far), y_last).wait_recv()

    def whole(g):
        return full[g].reshape(Y * ROWS, WIDTH)

    size = block[0]
    row_at = lax.broadcasted_iota(I32, (ROWS, WIDTH), 0) + y * ROWS
    col_at = lax.broadcasted_iota(I32, (ROWS, WIDTH), 1)
    inside = ((row_at < size) & (col_at < size)).astype(F32)
    cmap_row = cmap[...]
    perm[:, 0:WIDTH] = (
        lax.broadcasted_iota(I32, (WIDTH, WIDTH), 0) == cmap_row
    ).astype(F32).astype(BF16)
    perm[:, WIDTH:WIDE] = jnp.zeros((WIDTH, WIDE - WIDTH), BF16)

    omega_copy.wait()
    gen = gen_ref[...] * inside
    gen_ref[...] = gen
    send(G, permuted(gen, perm))
    ham_copy.wait()
    ham = ham_ref[...] * inside
    ham_ref[...] = ham
    send(H, permuted(ham, perm))
    full[YG, y] = gen.astype(BF16)
    full[YH, y] = ham.astype(BF16)
    pl.semaphore_wait(barrier, C - 1 + 2)
    start_out(G)
    y_send(YG)
    start_out(H)
    y_send(YH)

    exact = lax.Precision.HIGHEST

    def exact_dot(a, b, dims):
        return lax.dot_general(a, b, (dims, ((), ())), precision=exact, preferred_element_type=F32)

    jl = jnp.broadcast_to(jrow[...], (128, 128)).astype(F32)
    fam = jnp.broadcast_to(frow[...], (128, 128)).astype(F32)
    one_hot_t = (lax.broadcasted_iota(jnp.int32, (128, 128), 0).astype(F32) == jl).astype(F32)
    picked = exact_dot(sixj[...], one_hot_t, ((1,), (0,)))
    picked = exact_dot(one_hot_t.T, picked, ((1,), (0,)))
    mixing = picked * (fam == fam.T).astype(F32)
    mix_hi[...], mix_lo[...] = halves(mixing)
    reverse = mixing.T
    rev_hi[...], rev_lo[...] = halves(reverse)
    sq_hi[...], sq_lo[...] = halves(exact_dot(mixing, reverse, ((1,), (0,))))

    cmap_f = cmap_row.astype(F32)
    for b in range(5):
        span = min(128, WIDTH - 128 * b)
        piece = jnp.broadcast_to(cmap_f[:, 128 * b : 128 * b + span], (128, span)).T
        for k in range(5):
            span_k = min(128, WIDTH - 128 * k)
            at = (lax.broadcasted_iota(jnp.int32, (span, 128), 1) + 128 * k).astype(F32)
            unperm[128 * b : 128 * b + span, 128 * k : 128 * k + span_k] = (
                (piece == at).astype(F32).astype(BF16)[:, 0:span_k]
            )

    gen_s[...] = (gen_ref[...] * pair_w[...]).astype(BF16)
    ham_s[...] = (ham_ref[...] * pair_w[...]).astype(BF16)

    y_relay(YG)
    y_relay(YH)

    @pl.when(owns)
    def _():
        arrived(G)
        send_mixed(GB, times(mix_hi, mix_lo))
        arrived(H)
        send_mixed(HB, times(mix_hi, mix_lo))

    y_finish(YG)
    y_finish(YH)
    pp_ref[...] = dot(gen_s[...], whole(YH)) - dot(ham_s[...], whole(YG))
    send(PP, permuted(pp_ref[...], perm))
    start_out(PP)

    gc = take_block(GB)
    y_start(YGC, gc.astype(BF16))
    gc_s[...] = (gc * cross_w[...]).astype(BF16)
    hc = take_block(HB)
    y_start(YHC, hc.astype(BF16))
    hc_s[...] = (hc * cross_w[...]).astype(BF16)
    y_relay(YGC)
    y_relay(YHC)

    @pl.when(owns)
    def _():
        arrived(PP)
        comb_ref[...] = times(mix_hi, mix_lo)

    y_finish(YGC)
    y_finish(YHC)
    wide_ref[:, 512:WIDE] = jnp.zeros((ROWS, WIDE - 512), F32)
    wide_ref[:, 0:WIDTH] = dot(gc_s[...], whole(YHC)) - dot(hc_s[...], whole(YGC))
    send(CC, wide_ref[...])
    start_out(CC)

    @pl.when(owns)
    def _():
        arrived(CC)
        send_mixed(EB, comb_ref[...] + times(sq_hi, sq_lo))
        send_mixed(RB, times(rev_hi, rev_lo))

    ec = take_block(EB)
    y_start(YEC, ec.astype(BF16))
    hc_s[...] = (ec * cross_w[...]).astype(BF16)
    y_relay(YEC)
    y_finish(YEC)
    wide_ref[:, 0:WIDTH] = dot(gc_s[...], whole(YEC)) - dot(hc_s[...], whole(YGC))
    send(SO, wide_ref[...])
    start_out(SO)

    eta = pp_ref[...] + permuted(take_block(RB), unperm)
    eta_ref[...] = eta
    y_start(YE, eta.astype(BF16))
    ham_s[...] = (eta * pair_w[...]).astype(BF16)
    y_relay(YE)

    @pl.when(owns)
    def _():
        arrived(SO)
        send_mixed(SB, times(rev_hi, rev_lo))

    y_finish(YE)
    pp_ref[...] = dot(gen_s[...], whole(YE)) - dot(ham_s[...], whole(YG))
    second = pp_ref[...] + permuted(take_block(SB), unperm)
    out[...] = (ham_ref[...] + eta_ref[...] + 0.5 * second) * inside

    for t in range(5):
        wait_rows(os_ref.at[t], (OWNERS - 1) * PER, os_sem.at[t])

    @pl.when(idle)
    def _():
        for t in range(5):
            wait_rows(os_ref.at[t], PER, os_sem.at[t])

    @pl.when(owns)
    def _():
        for t in range(5):
            wait_rows(bs_ref.at[t], (C - 1) * PER, bs_sem.at[t])

    for g in range(6):
        y_copy(g, 0, own_rows(g, y), y_next).wait_send()
        y_copy(g, 1, own_rows(g, y), y_last).wait_send()
        y_copy(g, 2, upper(g, y_last), y_next).wait_send()
        y_copy(g, 3, lower(g, y_next), y_last).wait_send()


def on_device(omega, hamiltonian, pair_occ, cross_occ, block_size, jlabel, family, sixj, column_map):
    vmem = pl.BlockSpec(memory_space=pltpu.VMEM)
    hbm = pl.BlockSpec(memory_space=pltpu.MemorySpace.HBM)
    smem = pl.BlockSpec(memory_space=pltpu.SMEM)
    square = pltpu.VMEM((128, 128), BF16)
    rows_f = pltpu.VMEM((ROWS, WIDTH), F32)
    rows_b = pltpu.VMEM((ROWS, WIDTH), BF16)
    result = pl.pallas_call(
        kernel,
        out_shape=jax.ShapeDtypeStruct((ROWS, WIDTH), F32),
        in_specs=[hbm, hbm, vmem, vmem, smem, vmem, vmem, vmem, vmem],
        out_specs=vmem,
        scratch_shapes=[
            pltpu.VMEM((5, WORDS, 128), I32),
            pltpu.VMEM((5, C * PER, 128), I32),
            pltpu.VMEM((5, C * PER, 128), I32),
            pltpu.VMEM((5, WORDS, 128), I32),
            pltpu.VMEM((6, Y, ROWS, WIDTH), BF16),
            pltpu.VMEM((WIDTH, WIDE), BF16),
            pltpu.VMEM((WIDTH, WIDTH), BF16),
            square, square, square, square, square, square,
            pltpu.VMEM((ROWS, WIDE), F32),
            rows_f,
            pltpu.VMEM((72, 128), I32),
            pltpu.VMEM((C, 768), BF16),
            pltpu.VMEM((C, 768), BF16),
            rows_f, rows_f, rows_f,
            pltpu.VMEM((C, 768), F32),
            rows_b, rows_b, rows_b, rows_b,
            rows_f,
            pltpu.SemaphoreType.DMA((2,)),
            pltpu.SemaphoreType.DMA((5,)),
            pltpu.SemaphoreType.DMA((5,)),
            pltpu.SemaphoreType.DMA((5,)),
            pltpu.SemaphoreType.DMA((5,)),
            pltpu.SemaphoreType.DMA((6, 4)),
            pltpu.SemaphoreType.DMA((6, 4)),
        ],
        compiler_params=pltpu.CompilerParams(
            collective_id=0, has_side_effects=True, vmem_limit_bytes=48 * 1024 * 1024
        ),
    )(
        omega.reshape(ROWS, WIDTH),
        hamiltonian.reshape(ROWS, WIDTH),
        pair_occ,
        cross_occ,
        block_size,
        jlabel.reshape(1, 128),
        family.reshape(1, 128),
        sixj,
        column_map.reshape(1, WIDTH),
    )
    return result.reshape(1, ROWS, WIDTH)


def solution(mesh):
    in_specs = (
        P("chan", "blk", None),
        P("chan", "blk", None),
        P("chan", None),
        P("chan", None),
        P("chan"),
        P(),
        P(),
        P(),
        P(),
    )
    return jax.shard_map(
        on_device, mesh=mesh, in_specs=in_specs, out_specs=P("chan", "blk", None), check_vma=False
    )
```

```python
import math

import jax
import jax.numpy as jnp
from jax import lax
from jax.experimental import pallas as pl
from jax.experimental.pallas import tpu as pltpu
from jax.sharding import PartitionSpec as P

F32 = jnp.float32
BF16 = jnp.bfloat16
I32 = jnp.int32
MESH = pl.DeviceIdType.MESH

C = 128
L = 8
Y = 4
ROWS = 144
WIDTH = 576
WIDE = 640
PER = 3
OWNERS = 112
WORDS = OWNERS * PER
TAIL = 40
SPLIT = 184
LAST = 328
CUT_COL = 256

G, H, PP, CC, SO = range(5)
GB, HB, EB, RB, SB = range(5)
YG, YH, YGC, YHC, YE, YEC = range(6)

FLOOR = -126.0
OUT_TOP = (0.25, 6.0, 2.0**11, 2.0**26, 2.0**55)
BACK_TOP = (2.0**6, 2.0**11, 2.0**40, 2.0**34, 2.0**63)


def per_octave(top):
    return 32766.0 / (math.log2(top) - FLOOR)


def dot(a, b):
    return jnp.dot(a, b, preferred_element_type=F32)


def halves(value):
    high = value.astype(BF16)
    return high, (value - high.astype(F32)).astype(BF16)


def encode(value, top):
    scale = per_octave(top)
    size = jnp.maximum(jnp.abs(value), 2.0**FLOOR)
    code = jnp.minimum(jnp.round((jnp.log2(size) - FLOOR) * scale), 32767.0)
    return jnp.where(value < 0, -code, code).astype(I32)


def decode(code, top):
    value = code.astype(F32)
    size = jnp.exp2(jnp.abs(value) * (1.0 / per_octave(top)) + FLOOR)
    size = jnp.where(value < 0, -size, size)
    return jnp.where(value == 0, 0.0, size)


def pack(first, second):
    return lax.shift_left(first, 16) | (second & 0xFFFF)


def unpack(word):
    first = lax.shift_right_arithmetic(word, 16)
    return first, lax.shift_right_arithmetic(lax.shift_left(word, 16), 16)


def kernel(
    omega_hbm, ham_hbm, pair_hbm, cross_hbm, block, jrow_hbm, frow_hbm, sixj_hbm, cmap_hbm,
    out,
    os_ref, or_ref, bs_ref, br_ref,
    full_a, full_b, perm, unperm, mix_hi, mix_lo, rev_hi, rev_lo, sq_hi, sq_lo,
    wide_ref, block_ref, tail_ref, x_hi, x_lo,
    gen_ref, ham_ref, pp_ref, comb_ref, gen_s, ham_s, gc_s, hc_s, eta_ref,
    pair_w, cross_w, jrow, frow, sixj, cmap,
    in_sem, os_sem, or_sem, bs_sem, br_sem, ys_sem, yr_sem,
):
    me = lax.axis_index("chan")
    y = lax.axis_index("blk")
    z = me // L
    lane = lax.rem(me, L)
    place = lax.rem(lane - z - 1 + 3 * L, L)
    owns = place < L - 1
    idle = place == L - 1
    mine = z * (L - 1) + jnp.minimum(place, L - 2)
    idle_n = place // (L - 1)
    y_next = lax.rem(y + 1, Y)
    y_last = lax.rem(y + Y - 1, Y)

    barrier = pltpu.get_barrier_semaphore()

    def greet(step, _):
        to = lax.rem(me + step, C)
        pl.semaphore_signal(barrier, inc=1, device_id={"chan": to}, device_id_type=MESH)
        return 0

    lax.fori_loop(1, C, greet, 0)
    for other in (y_next, y_last):
        pl.semaphore_signal(barrier, inc=1, device_id={"blk": other}, device_id_type=MESH)

    pairs = (
        (cmap_hbm, cmap), (omega_hbm, gen_ref), (ham_hbm, ham_ref), (jrow_hbm, jrow),
        (frow_hbm, frow), (sixj_hbm, sixj), (pair_hbm, pair_w), (cross_hbm, cross_w),
    )
    loads = [pltpu.make_async_copy(a, b, in_sem.at[k]) for k, (a, b) in enumerate(pairs)]
    for load in loads:
        load.start()

    os_rows = os_ref.reshape(5, PER, OWNERS, 128)
    br_rows = br_ref.reshape(5, PER, OWNERS, 128)

    def pick(ref, t, j, n, index):
        return ref.at[t, pl.ds(j, n), pl.ds(index, 1)]

    def start_out(t, j, n):
        first = z * (L - 1) + place + 1 - idle_n

        def one(step, _):
            owner = lax.rem(first + step, OWNERS)
            plane = owner // (L - 1)
            to = plane * L + lax.rem(plane + 1 + lax.rem(owner, L - 1), L)
            pltpu.make_async_remote_copy(
                src_ref=pick(os_rows, t, j, n, owner), dst_ref=pick(or_ref, t, j, n, me),
                send_sem=os_sem.at[t, j], recv_sem=or_sem.at[t, j],
                device_id={"chan": to}, device_id_type=MESH,
            ).start()
            return 0

        lax.fori_loop(0, OWNERS - 1 + idle_n, one, 0)

        @pl.when(owns)
        def _():
            pltpu.make_async_copy(
                pick(os_rows, t, j, n, mine), pick(or_ref, t, j, n, me), or_sem.at[t, j]
            ).start()

    def start_back(t, j, n):
        def one(step, _):
            to = lax.rem(me + step, C)
            pltpu.make_async_remote_copy(
                src_ref=pick(bs_ref, t, j, n, to), dst_ref=pick(br_rows, t, j, n, mine),
                send_sem=bs_sem.at[t, j], recv_sem=br_sem.at[t, j],
                device_id={"chan": to}, device_id_type=MESH,
            ).start()
            return 0

        lax.fori_loop(1, C, one, 0)
        pltpu.make_async_copy(
            pick(bs_ref, t, j, n, me), pick(br_rows, t, j, n, mine), br_sem.at[t, j]
        ).start()

    def wait_rows(ref, t, j, n, count, sem):
        part = ref.at[t, pl.ds(j, n), pl.ds(0, count)]
        pltpu.make_async_copy(part, part, sem.at[t, j]).wait()

    def put_a(t, value):
        code = encode(value, OUT_TOP[t])
        tail_ref[...] = code[0:72, 256:384] + pltpu.roll(code[72:144, 256:384], 64, 1)
        os_ref[t, 0:TAIL, :] = pack(tail_ref[0:40, :], tail_ref[32:72, :])
        os_ref[t, TAIL:SPLIT, :] = pack(code[:, 0:128], code[:, 128:256])

    def put_b(t, value):
        code = encode(value, OUT_TOP[t])
        os_ref[t, SPLIT:LAST, :] = pack(code[:, 0:128], code[:, 128:256])
        os_ref[t, LAST:WORDS, :] = jnp.zeros((WORDS - LAST, 128), I32)

    def send(t, value):
        put_a(t, value[:, CUT_COL:WIDE])
        put_b(t, value[:, 0:CUT_COL])
        start_out(t, 0, PER)

    def arrived(t, j, n):
        wait_rows(or_ref, t, j, n, C, or_sem)
        for row in range(j, j + n):
            for k, code in enumerate(unpack(or_ref[t, row])):
                at = slice(256 * row + 128 * k, 256 * row + 128 * (k + 1))
                x_hi[:, at], x_lo[:, at] = halves(decode(code, OUT_TOP[t]))

    def times(high, low, j, n):
        at = slice(256 * j, 256 * (j + n))
        return dot(high[...], x_hi[:, at]) + (dot(high[...], x_lo[:, at]) + dot(low[...], x_hi[:, at]))

    def put_mixed(t, j, n, value):
        code = encode(value, BACK_TOP[t])
        for row in range(n):
            bs_ref[t, j + row] = pack(
                code[:, 256 * row : 256 * row + 128], code[:, 256 * row + 128 : 256 * row + 256]
            )

    def send_mixed(t, j, n, value):
        put_mixed(t, j, n, value)
        start_back(t, j, n)

    def back(t, j, n):
        wait_rows(br_rows, t, j, n, OWNERS, br_sem)

    def take_a(t):
        top = BACK_TOP[t]
        first, second = unpack(br_ref[t, 0:TAIL, :])
        tail_ref[0:40, :] = first
        tail_ref[32:72, :] = second
        tail = decode(tail_ref[...], top)
        block_ref[0:72, 512:576] = tail[:, 0:64]
        block_ref[72:144, 512:576] = pltpu.roll(tail, 64, 1)[:, 0:64]
        first, second = unpack(br_ref[t, TAIL:SPLIT, :])
        block_ref[:, 256:384] = decode(first, top)
        block_ref[:, 384:512] = decode(second, top)

    def take_b(t):
        top = BACK_TOP[t]
        first, second = unpack(br_ref[t, SPLIT:LAST, :])
        block_ref[:, 0:128] = decode(first, top)
        block_ref[:, 128:256] = decode(second, top)

    def permuted(value, matrix):
        high, low = halves(value)
        return dot(high, matrix[...]) + dot(low, matrix[...])

    CUT = 80
    parts = (full_a, full_b)

    def y_copy(g, c, k, rows, to):
        return pltpu.make_async_remote_copy(
            src_ref=rows, dst_ref=rows,
            send_sem=ys_sem.at[2 * g + c, k], recv_sem=yr_sem.at[2 * g + c, k],
            device_id={"blk": to}, device_id_type=MESH,
        )

    def own_rows(g, c, who):
        return parts[c].at[g, who]

    def upper(g, c, who):
        return parts[c].at[g, who, pl.ds(0, CUT)]

    def lower(g, c, who):
        return parts[c].at[g, who, pl.ds(CUT, ROWS - CUT)]

    def y_send(g, c):
        y_copy(g, c, 0, own_rows(g, c, y), y_next).start()
        y_copy(g, c, 1, own_rows(g, c, y), y_last).start()

    def y_start(g, c, value):
        parts[c][g, y] = value.astype(BF16)
        y_send(g, c)

    def y_relay(g, c):
        y_copy(g, c, 0, own_rows(g, c, y_last), y_next).wait_recv()
        y_copy(g, c, 2, upper(g, c, y_last), y_next).start()
        y_copy(g, c, 1, own_rows(g, c, y_next), y_last).wait_recv()
        y_copy(g, c, 3, lower(g, c, y_next), y_last).start()

    def y_finish(g, c):
        far = lax.rem(y + 2, Y)
        y_copy(g, c, 2, upper(g, c, far), y_next).wait_recv()
        y_copy(g, c, 3, lower(g, c, far), y_last).wait_recv()

    def whole(g, c):
        return parts[c][g].reshape(Y * ROWS, parts[c].shape[-1])

    size = block[0]
    row_at = lax.broadcasted_iota(I32, (ROWS, WIDTH), 0) + y * ROWS
    col_at = lax.broadcasted_iota(I32, (ROWS, WIDTH), 1)
    inside = ((row_at < size) & (col_at < size)).astype(F32)
    loads[0].wait()
    cmap_row = cmap[...].reshape(1, WIDTH)
    perm[:, 0:WIDTH] = (
        lax.broadcasted_iota(I32, (WIDTH, WIDTH), 0) == cmap_row
    ).astype(F32).astype(BF16)
    perm[:, WIDTH:WIDE] = jnp.zeros((WIDTH, WIDE - WIDTH), BF16)

    loads[1].wait()
    gen = gen_ref[...] * inside
    gen_ref[...] = gen
    value = permuted(gen, perm)
    put_a(G, value[:, CUT_COL:WIDE])
    put_b(G, value[:, 0:CUT_COL])
    full_a[YG, y] = gen[:, CUT_COL:].astype(BF16)
    full_b[YG, y] = gen[:, 0:CUT_COL].astype(BF16)
    pl.semaphore_wait(barrier, C - 1 + 2)
    start_out(G, 0, PER)
    loads[2].wait()
    ham = ham_ref[...] * inside
    ham_ref[...] = ham
    send(H, permuted(ham, perm))
    y_send(YG, 0)
    y_send(YG, 1)
    y_start(YH, 0, ham[:, CUT_COL:])
    y_start(YH, 1, ham[:, 0:CUT_COL])
    for load in loads[3:]:
        load.wait()

    exact = lax.Precision.HIGHEST

    def exact_dot(a, b, dims):
        return lax.dot_general(a, b, (dims, ((), ())), precision=exact, preferred_element_type=F32)

    jl = jnp.broadcast_to(jrow[...], (128, 128)).astype(F32)
    fam = jnp.broadcast_to(frow[...], (128, 128)).astype(F32)
    one_hot_t = (lax.broadcasted_iota(jnp.int32, (128, 128), 0).astype(F32) == jl).astype(F32)
    picked = exact_dot(sixj[...], one_hot_t, ((1,), (0,)))
    picked = exact_dot(one_hot_t.T, picked, ((1,), (0,)))
    mixing = picked * (fam == fam.T).astype(F32)
    mix_hi[...], mix_lo[...] = halves(mixing)
    reverse = mixing.T
    rev_hi[...], rev_lo[...] = halves(reverse)
    sq_hi[...], sq_lo[...] = halves(exact_dot(mixing, reverse, ((1,), (0,))))

    cmap_f = cmap_row.astype(F32)
    for b in range(5):
        span = min(128, WIDTH - 128 * b)
        piece = jnp.broadcast_to(cmap_f[:, 128 * b : 128 * b + span], (128, span)).T
        for k in range(5):
            span_k = min(128, WIDTH - 128 * k)
            at = (lax.broadcasted_iota(jnp.int32, (span, 128), 1) + 128 * k).astype(F32)
            unperm[128 * b : 128 * b + span, 128 * k : 128 * k + span_k] = (
                (piece == at).astype(F32).astype(BF16)[:, 0:span_k]
            )

    gen_s[...] = (gen_ref[...] * pair_w[...]).astype(BF16)
    ham_s[...] = (ham_ref[...] * pair_w[...]).astype(BF16)

    for g in (YG, YH):
        for c in range(2):
            y_relay(g, c)

    @pl.when(owns)
    def _():
        arrived(G, 0, PER)
        send_mixed(GB, 0, PER, times(mix_hi, mix_lo, 0, PER))
        arrived(H, 0, PER)
        put_mixed(HB, 0, PER, times(mix_hi, mix_lo, 0, PER))
        start_back(HB, 0, 2)
        start_back(HB, 2, 1)

    for g in (YG, YH):
        for c in range(2):
            y_finish(g, c)

    def commuted(first, second_full, second, first_full, c):
        return dot(first[...], whole(second_full, c)) - dot(second[...], whole(first_full, c))

    pp_ref[:, CUT_COL:] = commuted(gen_s, YH, ham_s, YG, 0)
    pp_ref[:, 0:CUT_COL] = commuted(gen_s, YH, ham_s, YG, 1)
    send(PP, permuted(pp_ref[...], perm))

    def take_and_gather(t, g):
        take_a(t)
        y_start(g, 0, block_ref[:, CUT_COL:])

    def take_rest(t, g):
        take_b(t)
        y_start(g, 1, block_ref[:, 0:CUT_COL])

    back(GB, 0, PER)
    take_and_gather(GB, YGC)
    take_rest(GB, YGC)
    gc_s[...] = (block_ref[...] * cross_w[...]).astype(BF16)
    y_relay(YGC, 0)
    y_relay(YGC, 1)
    back(HB, 0, 2)
    take_and_gather(HB, YHC)
    back(HB, 2, 1)
    take_rest(HB, YHC)
    hc_s[...] = (block_ref[...] * cross_w[...]).astype(BF16)
    y_relay(YHC, 0)
    y_relay(YHC, 1)

    @pl.when(owns)
    def _():
        arrived(PP, 0, PER)
        comb_ref[...] = times(mix_hi, mix_lo, 0, PER)

    wide_ref[:, 256:384] = jnp.zeros((ROWS, 128), F32)

    def cross_commutator(t, g):
        y_finish(g, 0)
        wide_ref[:, 0:320] = commuted(gc_s, g, hc_s, YGC, 0)
        put_a(t, wide_ref[...])
        start_out(t, 0, 1)
        y_finish(g, 1)
        put_b(t, commuted(gc_s, g, hc_s, YGC, 1))
        start_out(t, 1, 2)

    y_finish(YGC, 0)
    y_finish(YGC, 1)
    cross_commutator(CC, YHC)

    @pl.when(owns)
    def _():
        arrived(CC, 0, 1)
        send_mixed(EB, 0, 1, comb_ref[:, 0:256] + times(sq_hi, sq_lo, 0, 1))
        arrived(CC, 1, 2)
        put_mixed(EB, 1, 2, comb_ref[:, 256:768] + times(sq_hi, sq_lo, 1, 2))
        start_back(EB, 1, 1)
        start_back(EB, 2, 1)
        send_mixed(RB, 0, PER, times(rev_hi, rev_lo, 0, PER))

    back(EB, 0, 1)
    back(EB, 1, 1)
    take_and_gather(EB, YEC)
    back(EB, 2, 1)
    take_rest(EB, YEC)
    hc_s[...] = (block_ref[...] * cross_w[...]).astype(BF16)
    y_relay(YEC, 0)
    y_relay(YEC, 1)
    cross_commutator(SO, YEC)

    back(RB, 0, PER)
    take_a(RB)
    take_b(RB)
    eta = pp_ref[...] + permuted(block_ref[...], unperm)
    eta_ref[...] = eta
    y_start(YE, 0, eta[:, CUT_COL:])
    y_start(YE, 1, eta[:, 0:CUT_COL])
    ham_s[...] = (eta * pair_w[...]).astype(BF16)

    @pl.when(owns)
    def _():
        arrived(SO, 0, 1)
        send_mixed(SB, 0, 1, times(rev_hi, rev_lo, 0, 1))

    y_relay(YE, 0)
    y_relay(YE, 1)

    @pl.when(owns)
    def _():
        arrived(SO, 1, 2)
        send_mixed(SB, 1, 2, times(rev_hi, rev_lo, 1, 2))

    y_finish(YE, 0)
    y_finish(YE, 1)
    pp_ref[:, CUT_COL:] = commuted(gen_s, YE, ham_s, YG, 0)
    pp_ref[:, 0:CUT_COL] = commuted(gen_s, YE, ham_s, YG, 1)
    back(SB, 0, 1)
    back(SB, 1, 2)
    take_a(SB)
    take_b(SB)
    second = pp_ref[...] + permuted(block_ref[...], unperm)
    out[...] = (ham_ref[...] + eta_ref[...] + 0.5 * second) * inside

    out_cuts = ((G, 0, PER), (H, 0, PER), (PP, 0, PER), (CC, 0, 1), (CC, 1, 2), (SO, 0, 1), (SO, 1, 2))
    back_cuts = (
        (GB, 0, PER), (HB, 0, 2), (HB, 2, 1), (EB, 0, 1), (EB, 1, 1), (EB, 2, 1),
        (RB, 0, PER), (SB, 0, 1), (SB, 1, 2),
    )
    for cut in out_cuts:
        wait_rows(os_rows, *cut, OWNERS - 1, os_sem)

    @pl.when(idle)
    def _():
        for cut in out_cuts:
            wait_rows(os_rows, *cut, 1, os_sem)

    @pl.when(owns)
    def _():
        for cut in back_cuts:
            wait_rows(bs_ref, *cut, C - 1, bs_sem)

    for g in range(6):
        for c in range(2):
            y_copy(g, c, 0, own_rows(g, c, y), y_next).wait_send()
            y_copy(g, c, 1, own_rows(g, c, y), y_last).wait_send()
            y_copy(g, c, 2, upper(g, c, y_last), y_next).wait_send()
            y_copy(g, c, 3, lower(g, c, y_next), y_last).wait_send()


def on_device(omega, hamiltonian, pair_occ, cross_occ, block_size, jlabel, family, sixj, column_map):
    vmem = pl.BlockSpec(memory_space=pltpu.VMEM)
    hbm = pl.BlockSpec(memory_space=pltpu.MemorySpace.HBM)
    smem = pl.BlockSpec(memory_space=pltpu.SMEM)
    square = pltpu.VMEM((128, 128), BF16)
    rows_f = pltpu.VMEM((ROWS, WIDTH), F32)
    rows_b = pltpu.VMEM((ROWS, WIDTH), BF16)
    result = pl.pallas_call(
        kernel,
        out_shape=jax.ShapeDtypeStruct((ROWS, WIDTH), F32),
        in_specs=[hbm, hbm, hbm, hbm, smem, hbm, hbm, hbm, hbm],
        out_specs=vmem,
        scratch_shapes=[
            pltpu.VMEM((5, WORDS, 128), I32),
            pltpu.VMEM((5, PER, C, 128), I32),
            pltpu.VMEM((5, PER, C, 128), I32),
            pltpu.VMEM((5, WORDS, 128), I32),
            pltpu.VMEM((6, Y, ROWS, WIDTH - CUT_COL), BF16),
            pltpu.VMEM((6, Y, ROWS, CUT_COL), BF16),
            pltpu.VMEM((WIDTH, WIDE), BF16),
            pltpu.VMEM((WIDTH, WIDTH), BF16),
            square, square, square, square, square, square,
            pltpu.VMEM((ROWS, WIDE - CUT_COL), F32),
            rows_f,
            pltpu.VMEM((72, 128), I32),
            pltpu.VMEM((C, 768), BF16),
            pltpu.VMEM((C, 768), BF16),
            rows_f, rows_f, rows_f,
            pltpu.VMEM((C, 768), F32),
            rows_b, rows_b, rows_b, rows_b,
            rows_f,
            pltpu.VMEM((1, WIDTH), F32),
            pltpu.VMEM((1, WIDTH), F32),
            pltpu.VMEM((1, 128), I32),
            pltpu.VMEM((1, 128), I32),
            pltpu.VMEM((128, 128), F32),
            pltpu.VMEM((WIDTH,), I32),
            pltpu.SemaphoreType.DMA((8,)),
            pltpu.SemaphoreType.DMA((5, PER)),
            pltpu.SemaphoreType.DMA((5, PER)),
            pltpu.SemaphoreType.DMA((5, PER)),
            pltpu.SemaphoreType.DMA((5, PER)),
            pltpu.SemaphoreType.DMA((12, 4)),
            pltpu.SemaphoreType.DMA((12, 4)),
        ],
        compiler_params=pltpu.CompilerParams(
            collective_id=0, has_side_effects=True, vmem_limit_bytes=60 * 1024 * 1024
        ),
    )(
        omega.reshape(ROWS, WIDTH),
        hamiltonian.reshape(ROWS, WIDTH),
        pair_occ,
        cross_occ,
        block_size,
        jlabel.reshape(1, 128),
        family.reshape(1, 128),
        sixj,
        column_map,
    )
    return result.reshape(1, ROWS, WIDTH)


def solution(mesh):
    in_specs = (
        P("chan", "blk", None),
        P("chan", "blk", None),
        P("chan", None),
        P("chan", None),
        P("chan"),
        P(),
        P(),
        P(),
        P(),
    )
    return jax.shard_map(
        on_device, mesh=mesh, in_specs=in_specs, out_specs=P("chan", "blk", None), check_vma=False
    )
```

```python
import math

import jax
import jax.numpy as jnp
from jax import lax
from jax.experimental import pallas as pl
from jax.experimental.pallas import tpu as pltpu
from jax.sharding import PartitionSpec as P

F32 = jnp.float32
BF16 = jnp.bfloat16
I32 = jnp.int32
MESH = pl.DeviceIdType.MESH

C = 128
L = 8
Y = 4
ROWS = 144
WIDTH = 576
WIDE = 640
PER = 3
OWNERS = 112
WORDS = OWNERS * PER
TAIL = 40
SPLIT = 184
LAST = 328
CUT_COL = 256

G, H, PP, CC, SO = range(5)
GB, HB, EB, RB, SB = range(5)
YG, YH, YGC, YHC, YE, YEC = range(6)

FLOOR = -126.0
OUT_TOP = (0.25, 6.0, 2.0**11, 2.0**26, 2.0**55)
BACK_TOP = (2.0**6, 2.0**11, 2.0**40, 2.0**34, 2.0**63)


def per_octave(top):
    return 32766.0 / (math.log2(top) - FLOOR)


def dot(a, b):
    return jnp.dot(a, b, preferred_element_type=F32)


def halves(value):
    high = value.astype(BF16)
    return high, (value - high.astype(F32)).astype(BF16)


def encode(value, top):
    scale = per_octave(top)
    size = jnp.maximum(jnp.abs(value), 2.0**FLOOR)
    code = jnp.minimum(jnp.round((jnp.log2(size) - FLOOR) * scale), 32767.0)
    return jnp.where(value < 0, -code, code).astype(I32)


def decode(code, top):
    value = code.astype(F32)
    size = jnp.exp2(jnp.abs(value) * (1.0 / per_octave(top)) + FLOOR)
    size = jnp.where(value < 0, -size, size)
    return jnp.where(value == 0, 0.0, size)


def pack(first, second):
    return lax.shift_left(first, 16) | (second & 0xFFFF)


def unpack(word):
    first = lax.shift_right_arithmetic(word, 16)
    return first, lax.shift_right_arithmetic(lax.shift_left(word, 16), 16)


def kernel(
    omega_hbm, ham_hbm, pair_hbm, cross_hbm, block, jrow_hbm, frow_hbm, sixj_hbm, cmap_hbm,
    out,
    os_ref, or_ref, bs_ref, br_ref,
    full_a, full_b, perm, unperm, mix_hi, mix_lo, rev_hi, rev_lo, sq_hi, sq_lo,
    wide_ref, block_ref, tail_ref, x_hi, x_lo,
    gen_ref, ham_ref, pp_ref, comb_ref, gen_s, ham_s, gc_s, hc_s, eta_ref,
    pair_w, cross_w, jrow, frow, sixj, cmap,
    in_sem, os_sem, or_sem, bs_sem, br_sem, ys_sem, yr_sem,
):
    me = lax.axis_index("chan")
    y = lax.axis_index("blk")
    z = me // L
    lane = lax.rem(me, L)
    place = lax.rem(lane - z - 1 + 3 * L, L)
    owns = place < L - 1
    idle = place == L - 1
    mine = z * (L - 1) + jnp.minimum(place, L - 2)
    idle_n = place // (L - 1)
    y_next = lax.rem(y + 1, Y)
    y_last = lax.rem(y + Y - 1, Y)

    barrier = pltpu.get_barrier_semaphore()

    def far_first(step, middle):
        half = (step + 1) // 2
        return middle + jnp.where(lax.rem(step, 2) == 1, half, -half)

    def greet(step, _):
        to = lax.rem(me + far_first(step, C // 2), C)
        pl.semaphore_signal(barrier, inc=1, device_id={"chan": to}, device_id_type=MESH)
        return 0

    lax.fori_loop(0, C - 1, greet, 0)
    for other in (y_next, y_last):
        pl.semaphore_signal(barrier, inc=1, device_id={"blk": other}, device_id_type=MESH)

    pairs = (
        (cmap_hbm, cmap), (omega_hbm, gen_ref), (ham_hbm, ham_ref), (jrow_hbm, jrow),
        (frow_hbm, frow), (sixj_hbm, sixj), (pair_hbm, pair_w), (cross_hbm, cross_w),
    )
    loads = [pltpu.make_async_copy(a, b, in_sem.at[k]) for k, (a, b) in enumerate(pairs)]
    for load in loads:
        load.start()

    os_rows = os_ref.reshape(5, PER, OWNERS, 128)
    br_rows = br_ref.reshape(5, PER, OWNERS, 128)

    def pick(ref, t, j, n, index):
        return ref.at[t, pl.ds(j, n), pl.ds(index, 1)]

    def start_out(t, j, n):
        first = z * (L - 1) + place

        def one(step, _):
            owner = lax.rem(first + far_first(step, OWNERS // 2), OWNERS)
            plane = owner // (L - 1)
            to = plane * L + lax.rem(plane + 1 + lax.rem(owner, L - 1), L)
            pltpu.make_async_remote_copy(
                src_ref=pick(os_rows, t, j, n, owner), dst_ref=pick(or_ref, t, j, n, me),
                send_sem=os_sem.at[t, j], recv_sem=or_sem.at[t, j],
                device_id={"chan": to}, device_id_type=MESH,
            ).start()
            return 0

        lax.fori_loop(0, OWNERS - 1 + idle_n, one, 0)

        @pl.when(owns)
        def _():
            pltpu.make_async_copy(
                pick(os_rows, t, j, n, mine), pick(or_ref, t, j, n, me), or_sem.at[t, j]
            ).start()

    def start_back(t, j, n):
        def one(step, _):
            to = lax.rem(me + far_first(step, C // 2), C)
            pltpu.make_async_remote_copy(
                src_ref=pick(bs_ref, t, j, n, to), dst_ref=pick(br_rows, t, j, n, mine),
                send_sem=bs_sem.at[t, j], recv_sem=br_sem.at[t, j],
                device_id={"chan": to}, device_id_type=MESH,
            ).start()
            return 0

        lax.fori_loop(0, C - 1, one, 0)
        pltpu.make_async_copy(
            pick(bs_ref, t, j, n, me), pick(br_rows, t, j, n, mine), br_sem.at[t, j]
        ).start()

    def wait_rows(ref, t, j, n, count, sem):
        part = ref.at[t, pl.ds(j, n), pl.ds(0, count)]
        pltpu.make_async_copy(part, part, sem.at[t, j]).wait()

    def put_a(t, value):
        code = encode(value, OUT_TOP[t])
        tail_ref[...] = code[0:72, 256:384] + pltpu.roll(code[72:144, 256:384], 64, 1)
        os_ref[t, 0:TAIL, :] = pack(tail_ref[0:40, :], tail_ref[32:72, :])
        os_ref[t, TAIL:SPLIT, :] = pack(code[:, 0:128], code[:, 128:256])

    def put_b(t, value):
        code = encode(value, OUT_TOP[t])
        os_ref[t, SPLIT:LAST, :] = pack(code[:, 0:128], code[:, 128:256])
        os_ref[t, LAST:WORDS, :] = jnp.zeros((WORDS - LAST, 128), I32)

    def send(t, value):
        put_a(t, value[:, CUT_COL:WIDE])
        put_b(t, value[:, 0:CUT_COL])
        start_out(t, 0, PER)

    def arrived(t, j, n):
        wait_rows(or_ref, t, j, n, C, or_sem)
        for row in range(j, j + n):
            for k, code in enumerate(unpack(or_ref[t, row])):
                at = slice(256 * row + 128 * k, 256 * row + 128 * (k + 1))
                x_hi[:, at], x_lo[:, at] = halves(decode(code, OUT_TOP[t]))

    def times(high, low, j, n):
        at = slice(256 * j, 256 * (j + n))
        return dot(high[...], x_hi[:, at]) + (dot(high[...], x_lo[:, at]) + dot(low[...], x_hi[:, at]))

    def put_mixed(t, j, n, value):
        code = encode(value, BACK_TOP[t])
        for row in range(n):
            bs_ref[t, j + row] = pack(
                code[:, 256 * row : 256 * row + 128], code[:, 256 * row + 128 : 256 * row + 256]
            )

    def send_mixed(t, j, n, value):
        put_mixed(t, j, n, value)
        start_back(t, j, n)

    def back(t, j, n):
        wait_rows(br_rows, t, j, n, OWNERS, br_sem)

    def take_a(t):
        top = BACK_TOP[t]
        first, second = unpack(br_ref[t, 0:TAIL, :])
        tail_ref[0:40, :] = first
        tail_ref[32:72, :] = second
        tail = decode(tail_ref[...], top)
        block_ref[0:72, 512:576] = tail[:, 0:64]
        block_ref[72:144, 512:576] = pltpu.roll(tail, 64, 1)[:, 0:64]
        first, second = unpack(br_ref[t, TAIL:SPLIT, :])
        block_ref[:, 256:384] = decode(first, top)
        block_ref[:, 384:512] = decode(second, top)

    def take_b(t):
        top = BACK_TOP[t]
        first, second = unpack(br_ref[t, SPLIT:LAST, :])
        block_ref[:, 0:128] = decode(first, top)
        block_ref[:, 128:256] = decode(second, top)

    def permuted(value, matrix):
        high, low = halves(value)
        return dot(high, matrix[...]) + dot(low, matrix[...])

    CUT = 80
    parts = (full_a, full_b)

    def y_copy(g, c, k, rows, to):
        return pltpu.make_async_remote_copy(
            src_ref=rows, dst_ref=rows,
            send_sem=ys_sem.at[2 * g + c, k], recv_sem=yr_sem.at[2 * g + c, k],
            device_id={"blk": to}, device_id_type=MESH,
        )

    def own_rows(g, c, who):
        return parts[c].at[g, who]

    def upper(g, c, who):
        return parts[c].at[g, who, pl.ds(0, CUT)]

    def lower(g, c, who):
        return parts[c].at[g, who, pl.ds(CUT, ROWS - CUT)]

    def y_send(g, c):
        y_copy(g, c, 0, own_rows(g, c, y), y_next).start()
        y_copy(g, c, 1, own_rows(g, c, y), y_last).start()

    def y_start(g, c, value):
        parts[c][g, y] = value.astype(BF16)
        y_send(g, c)

    def y_relay(g, c):
        y_copy(g, c, 0, own_rows(g, c, y_last), y_next).wait_recv()
        y_copy(g, c, 2, upper(g, c, y_last), y_next).start()
        y_copy(g, c, 1, own_rows(g, c, y_next), y_last).wait_recv()
        y_copy(g, c, 3, lower(g, c, y_next), y_last).start()

    def y_finish(g, c):
        far = lax.rem(y + 2, Y)
        y_copy(g, c, 2, upper(g, c, far), y_next).wait_recv()
        y_copy(g, c, 3, lower(g, c, far), y_last).wait_recv()

    def whole(g, c):
        return parts[c][g].reshape(Y * ROWS, parts[c].shape[-1])

    size = block[0]
    row_at = lax.broadcasted_iota(I32, (ROWS, WIDTH), 0) + y * ROWS
    col_at = lax.broadcasted_iota(I32, (ROWS, WIDTH), 1)
    inside = ((row_at < size) & (col_at < size)).astype(F32)
    loads[0].wait()
    cmap_row = cmap[...].reshape(1, WIDTH)
    perm[:, 0:WIDTH] = (
        lax.broadcasted_iota(I32, (WIDTH, WIDTH), 0) == cmap_row
    ).astype(F32).astype(BF16)
    perm[:, WIDTH:WIDE] = jnp.zeros((WIDTH, WIDE - WIDTH), BF16)

    loads[1].wait()
    gen = gen_ref[...] * inside
    gen_ref[...] = gen
    value = permuted(gen, perm)
    put_a(G, value[:, CUT_COL:WIDE])
    put_b(G, value[:, 0:CUT_COL])
    full_a[YG, y] = gen[:, CUT_COL:].astype(BF16)
    full_b[YG, y] = gen[:, 0:CUT_COL].astype(BF16)
    pl.semaphore_wait(barrier, C - 1 + 2)
    start_out(G, 0, PER)
    loads[2].wait()
    ham = ham_ref[...] * inside
    ham_ref[...] = ham
    send(H, permuted(ham, perm))
    y_send(YG, 0)
    y_send(YG, 1)
    y_start(YH, 0, ham[:, CUT_COL:])
    y_start(YH, 1, ham[:, 0:CUT_COL])
    for load in loads[3:]:
        load.wait()

    exact = lax.Precision.HIGHEST

    def exact_dot(a, b, dims):
        return lax.dot_general(a, b, (dims, ((), ())), precision=exact, preferred_element_type=F32)

    jl = jnp.broadcast_to(jrow[...], (128, 128)).astype(F32)
    fam = jnp.broadcast_to(frow[...], (128, 128)).astype(F32)
    one_hot_t = (lax.broadcasted_iota(jnp.int32, (128, 128), 0).astype(F32) == jl).astype(F32)
    picked = exact_dot(sixj[...], one_hot_t, ((1,), (0,)))
    picked = exact_dot(one_hot_t.T, picked, ((1,), (0,)))
    mixing = picked * (fam == fam.T).astype(F32)
    mix_hi[...], mix_lo[...] = halves(mixing)
    reverse = mixing.T
    rev_hi[...], rev_lo[...] = halves(reverse)
    sq_hi[...], sq_lo[...] = halves(exact_dot(mixing, reverse, ((1,), (0,))))

    cmap_f = cmap_row.astype(F32)
    for b in range(5):
        span = min(128, WIDTH - 128 * b)
        piece = jnp.broadcast_to(cmap_f[:, 128 * b : 128 * b + span], (128, span)).T
        for k in range(5):
            span_k = min(128, WIDTH - 128 * k)
            at = (lax.broadcasted_iota(jnp.int32, (span, 128), 1) + 128 * k).astype(F32)
            unperm[128 * b : 128 * b + span, 128 * k : 128 * k + span_k] = (
                (piece == at).astype(F32).astype(BF16)[:, 0:span_k]
            )

    gen_s[...] = (gen_ref[...] * pair_w[...]).astype(BF16)
    ham_s[...] = (ham_ref[...] * pair_w[...]).astype(BF16)

    for g in (YG, YH):
        for c in range(2):
            y_relay(g, c)

    @pl.when(owns)
    def _():
        arrived(G, 0, PER)
        send_mixed(GB, 0, PER, times(mix_hi, mix_lo, 0, PER))
        arrived(H, 0, PER)
        put_mixed(HB, 0, PER, times(mix_hi, mix_lo, 0, PER))
        start_back(HB, 0, 2)
        start_back(HB, 2, 1)

    for g in (YG, YH):
        for c in range(2):
            y_finish(g, c)

    def commuted(first, second_full, second, first_full, c):
        return dot(first[...], whole(second_full, c)) - dot(second[...], whole(first_full, c))

    pp_ref[:, CUT_COL:] = commuted(gen_s, YH, ham_s, YG, 0)
    pp_ref[:, 0:CUT_COL] = commuted(gen_s, YH, ham_s, YG, 1)
    send(PP, permuted(pp_ref[...], perm))

    def take_and_gather(t, g):
        take_a(t)
        y_start(g, 0, block_ref[:, CUT_COL:])

    def take_rest(t, g):
        take_b(t)
        y_start(g, 1, block_ref[:, 0:CUT_COL])

    back(GB, 0, PER)
    take_and_gather(GB, YGC)
    take_rest(GB, YGC)
    gc_s[...] = (block_ref[...] * cross_w[...]).astype(BF16)
    y_relay(YGC, 0)
    y_relay(YGC, 1)
    back(HB, 0, 2)
    take_and_gather(HB, YHC)
    back(HB, 2, 1)
    take_rest(HB, YHC)
    hc_s[...] = (block_ref[...] * cross_w[...]).astype(BF16)
    y_relay(YHC, 0)
    y_relay(YHC, 1)

    @pl.when(owns)
    def _():
        arrived(PP, 0, PER)
        comb_ref[...] = times(mix_hi, mix_lo, 0, PER)

    wide_ref[:, 256:384] = jnp.zeros((ROWS, 128), F32)

    def cross_commutator(t, g):
        wide_ref[:, 0:320] = dot(hc_s[...], whole(YGC, 0))
        block_ref[:, 0:CUT_COL] = dot(hc_s[...], whole(YGC, 1))
        y_finish(g, 0)
        wide_ref[:, 0:320] = dot(gc_s[...], whole(g, 0)) - wide_ref[:, 0:320]
        put_a(t, wide_ref[...])
        start_out(t, 0, 1)
        y_finish(g, 1)
        put_b(t, dot(gc_s[...], whole(g, 1)) - block_ref[:, 0:CUT_COL])
        start_out(t, 1, 2)

    y_finish(YGC, 0)
    y_finish(YGC, 1)
    cross_commutator(CC, YHC)

    @pl.when(owns)
    def _():
        arrived(CC, 0, 1)
        send_mixed(EB, 0, 1, comb_ref[:, 0:256] + times(sq_hi, sq_lo, 0, 1))
        arrived(CC, 1, 2)
        put_mixed(EB, 1, 2, comb_ref[:, 256:768] + times(sq_hi, sq_lo, 1, 2))
        start_back(EB, 1, 1)
        start_back(EB, 2, 1)
        send_mixed(RB, 0, PER, times(rev_hi, rev_lo, 0, PER))

    back(EB, 0, 1)
    back(EB, 1, 1)
    take_and_gather(EB, YEC)
    back(EB, 2, 1)
    take_rest(EB, YEC)
    hc_s[...] = (block_ref[...] * cross_w[...]).astype(BF16)
    y_relay(YEC, 0)
    y_relay(YEC, 1)
    cross_commutator(SO, YEC)

    back(RB, 0, PER)
    take_a(RB)
    take_b(RB)
    eta = pp_ref[...] + permuted(block_ref[...], unperm)
    eta_ref[...] = eta
    y_start(YE, 0, eta[:, CUT_COL:])
    y_start(YE, 1, eta[:, 0:CUT_COL])
    ham_s[...] = (eta * pair_w[...]).astype(BF16)

    @pl.when(owns)
    def _():
        arrived(SO, 0, 1)
        send_mixed(SB, 0, 1, times(rev_hi, rev_lo, 0, 1))

    y_relay(YE, 0)
    y_relay(YE, 1)

    @pl.when(owns)
    def _():
        arrived(SO, 1, 2)
        send_mixed(SB, 1, 2, times(rev_hi, rev_lo, 1, 2))

    y_finish(YE, 0)
    y_finish(YE, 1)
    pp_ref[:, CUT_COL:] = commuted(gen_s, YE, ham_s, YG, 0)
    pp_ref[:, 0:CUT_COL] = commuted(gen_s, YE, ham_s, YG, 1)
    back(SB, 0, 1)
    back(SB, 1, 2)
    take_a(SB)
    take_b(SB)
    second = pp_ref[...] + permuted(block_ref[...], unperm)
    out[...] = (ham_ref[...] + eta_ref[...] + 0.5 * second) * inside

    out_cuts = ((G, 0, PER), (H, 0, PER), (PP, 0, PER), (CC, 0, 1), (CC, 1, 2), (SO, 0, 1), (SO, 1, 2))
    back_cuts = (
        (GB, 0, PER), (HB, 0, 2), (HB, 2, 1), (EB, 0, 1), (EB, 1, 1), (EB, 2, 1),
        (RB, 0, PER), (SB, 0, 1), (SB, 1, 2),
    )
    for cut in out_cuts:
        wait_rows(os_rows, *cut, OWNERS - 1, os_sem)

    @pl.when(idle)
    def _():
        for cut in out_cuts:
            wait_rows(os_rows, *cut, 1, os_sem)

    @pl.when(owns)
    def _():
        for cut in back_cuts:
            wait_rows(bs_ref, *cut, C - 1, bs_sem)

    for g in range(6):
        for c in range(2):
            y_copy(g, c, 0, own_rows(g, c, y), y_next).wait_send()
            y_copy(g, c, 1, own_rows(g, c, y), y_last).wait_send()
            y_copy(g, c, 2, upper(g, c, y_last), y_next).wait_send()
            y_copy(g, c, 3, lower(g, c, y_next), y_last).wait_send()


def on_device(omega, hamiltonian, pair_occ, cross_occ, block_size, jlabel, family, sixj, column_map):
    vmem = pl.BlockSpec(memory_space=pltpu.VMEM)
    hbm = pl.BlockSpec(memory_space=pltpu.MemorySpace.HBM)
    smem = pl.BlockSpec(memory_space=pltpu.SMEM)
    square = pltpu.VMEM((128, 128), BF16)
    rows_f = pltpu.VMEM((ROWS, WIDTH), F32)
    rows_b = pltpu.VMEM((ROWS, WIDTH), BF16)
    result = pl.pallas_call(
        kernel,
        out_shape=jax.ShapeDtypeStruct((ROWS, WIDTH), F32),
        in_specs=[hbm, hbm, hbm, hbm, smem, hbm, hbm, hbm, hbm],
        out_specs=vmem,
        scratch_shapes=[
            pltpu.VMEM((5, WORDS, 128), I32),
            pltpu.VMEM((5, PER, C, 128), I32),
            pltpu.VMEM((5, PER, C, 128), I32),
            pltpu.VMEM((5, WORDS, 128), I32),
            pltpu.VMEM((6, Y, ROWS, WIDTH - CUT_COL), BF16),
            pltpu.VMEM((6, Y, ROWS, CUT_COL), BF16),
            pltpu.VMEM((WIDTH, WIDE), BF16),
            pltpu.VMEM((WIDTH, WIDTH), BF16),
            square, square, square, square, square, square,
            pltpu.VMEM((ROWS, WIDE - CUT_COL), F32),
            rows_f,
            pltpu.VMEM((72, 128), I32),
            pltpu.VMEM((C, 768), BF16),
            pltpu.VMEM((C, 768), BF16),
            rows_f, rows_f, rows_f,
            pltpu.VMEM((C, 768), F32),
            rows_b, rows_b, rows_b, rows_b,
            rows_f,
            pltpu.VMEM((1, WIDTH), F32),
            pltpu.VMEM((1, WIDTH), F32),
            pltpu.VMEM((1, 128), I32),
            pltpu.VMEM((1, 128), I32),
            pltpu.VMEM((128, 128), F32),
            pltpu.VMEM((WIDTH,), I32),
            pltpu.SemaphoreType.DMA((8,)),
            pltpu.SemaphoreType.DMA((5, PER)),
            pltpu.SemaphoreType.DMA((5, PER)),
            pltpu.SemaphoreType.DMA((5, PER)),
            pltpu.SemaphoreType.DMA((5, PER)),
            pltpu.SemaphoreType.DMA((12, 4)),
            pltpu.SemaphoreType.DMA((12, 4)),
        ],
        compiler_params=pltpu.CompilerParams(
            collective_id=0, has_side_effects=True, vmem_limit_bytes=60 * 1024 * 1024
        ),
    )(
        omega.reshape(ROWS, WIDTH),
        hamiltonian.reshape(ROWS, WIDTH),
        pair_occ,
        cross_occ,
        block_size,
        jlabel.reshape(1, 128),
        family.reshape(1, 128),
        sixj,
        column_map,
    )
    return result.reshape(1, ROWS, WIDTH)


def solution(mesh):
    in_specs = (
        P("chan", "blk", None),
        P("chan", "blk", None),
        P("chan", None),
        P("chan", None),
        P("chan"),
        P(),
        P(),
        P(),
        P(),
    )
    return jax.shard_map(
        on_device, mesh=mesh, in_specs=in_specs, out_specs=P("chan", "blk", None), check_vma=False
    )
```
